32 devices in a mesh: rep: 2 (over y), gx: 4 (over z), gy: 2 (over x), gz: 2 (over core).
Axes of the slice: x: 2, y: 2, z: 4, core: 2. Of those that a mesh axis runs over, the one named last changes fastest.
Arguments:
- tokens: bfloat16 [1024, 8192], P('rep', ('gx', 'gy', 'gz')), parts along dimension 0, may hold values from -6 to 6
- gate_weight: bfloat16 [8192, 26624], P('gx', ('gy', 'gz')), may hold values from -0.0625 to 0.0625
- up_weight: bfloat16 [8192, 26624], P('gx', ('gy', 'gz')), may hold values from -0.0625 to 0.0625
- down_weight: bfloat16 [26624, 8192], P(('gy', 'gz'), 'gx'), may hold values from -0.0546875 to 0.0546875
Outputs:
- ffn_output: bfloat16 [1024, 8192], P('rep', ('gx', 'gy', 'gz')), parts along dimension 0
The draws below stay inside these ranges and needn't reach their ends.
There are 2 independent parts, one for each index of `rep`. The reference program is written for one: setup_inputs(seed, part) draws one part's arguments, and reference() takes and returns one part's arrays. A program takes and returns all parts, laid end to end along the dimension named above; an argument that names none is the same for every part. Nothing has to cross between parts.
All inputs are finite; a program needn't handle non-finite values.
Results may differ from the reference program's by a relative error of at most 0.019.
Values may be sent and summed in bfloat16 or wider, within the bound.
A program may use at most 256 MiB of HBM per device.

```python
import jax
import jax.numpy as jnp
from jax import lax

D = 8192
FF = 26624
TOKENS = 512
N_GX = 4


def spiked(values, rng, source, target, blocks, factor):
    def block_of(axis_at):
        return (jnp.arange(values.shape[axis_at]) // (values.shape[axis_at] // blocks)).reshape((-1,) + (1,) * (values.ndim - 1 - axis_at))

    first = jax.random.permutation(rng, blocks)[block_of(target)]
    far = (block_of(target) + blocks // 2) % blocks
    return jnp.where((block_of(source) == first) | (block_of(source) == far), factor * values, values)


def steps_of(key, shape, split, least, top_value):
    def one(axis_at, shards_of):
        heights = jax.random.uniform(jax.random.fold_in(jax.random.fold_in(key, 6), axis_at), (shards_of,), jnp.float32, least / len(split), top_value / len(split))
        return jnp.repeat(jnp.exp(heights), shape[axis_at] // shards_of).reshape((-1,) + (1,) * (len(shape) - axis_at - 1))

    level = one(*split[0])
    for cut in split[1:]:
        level = level * one(*cut)
    return level


def bell_draw(rng, dims, spread, bound, shards=(), kind=jnp.bfloat16):
    entries = spread * jax.random.normal(rng, dims, jnp.float32)
    if shards:
        entries = entries * steps_of(rng, dims, shards, -0.22, 0.18)
    return jnp.clip(entries, -bound, bound).astype(kind)


def gaussian_with(rng, shape, width, reach, cuts, heavy, held_as=jnp.bfloat16):
    result = width * jax.random.normal(rng, shape, jnp.float32)
    if cuts:
        result = result * steps_of(rng, shape, cuts, -0.22, 0.18)
    return jnp.clip(spiked(result, jax.random.fold_in(rng, 3), *heavy), -reach, reach).astype(held_as)


def setup_inputs(seed: int = 0, part: int = 0) -> dict:
    arg_keys = jax.random.split(jax.random.key(seed), 5)
    part_splits = jax.random.split(jax.random.fold_in(arg_keys[4], part), 5)
    return {
        "tokens": gaussian_with(part_splits[0], (TOKENS, D), 1.0, 6.0, ((1, 16),), (1, 0, 16, 2.0)),
        "gate_weight": bell_draw(arg_keys[1], (D, FF), D ** -0.5, 0.0625, ((0, 4), (1, 4))),
        "up_weight": bell_draw(arg_keys[2], (D, FF), D ** -0.5, 0.0625, ((0, 4), (1, 4))),
        "down_weight": gaussian_with(arg_keys[3], (FF, D), FF ** -0.5, 0.0546875, ((0, 4), (1, 4)), (0, 1, 4, 2.0)),
    }


def rounded(values):
    return lax.optimization_barrier(values.astype(jnp.bfloat16)).astype(jnp.float32)


def reference(tokens, gate_weight, up_weight, down_weight):
    block_width = D // N_GX

    def add_block(block_index, totals):
        offset = (block_index * block_width).astype(jnp.int32)
        tok_cols = lax.dynamic_slice_in_dim(tokens, offset, block_width, 1)
        gate_rows = lax.dynamic_slice_in_dim(gate_weight, offset, block_width, 0)
        up_rows = lax.dynamic_slice_in_dim(up_weight, offset, block_width, 0)
        gate_part = rounded(jnp.dot(tok_cols, gate_rows, preferred_element_type=jnp.float32))
        up_part = rounded(jnp.dot(tok_cols, up_rows, preferred_element_type=jnp.float32))
        return (totals[0] + gate_part, totals[1] + up_part)

    initial = jnp.zeros((TOKENS, FF), jnp.float32)
    gate_sum, up_sum = lax.fori_loop(jnp.int32(0), jnp.int32(N_GX), add_block, (initial, initial))
    hidden = (jax.nn.silu(gate_sum) * up_sum).astype(jnp.bfloat16)
    return jnp.dot(hidden, down_weight, preferred_element_type=jnp.float32).astype(jnp.bfloat16)
```

```python
import functools

import jax
import jax.numpy as jnp
from jax import lax
from jax.experimental import pallas as pl
from jax.experimental.pallas import tpu as pltpu
from jax.sharding import PartitionSpec as P

MESH = pl.DeviceIdType.MESH
WIDE = 128
LAG = 2
F32, BF16 = jnp.float32, jnp.bfloat16


def both(low, value, high):
    return jnp.logical_and(value >= low, value < high)


def kernel(
    n, count, pair, tok, gate, up, down, out,
    part, got, hid, acc, wbuf, dbuf,
    psend, precv, hsend, hrecv, wsem, dsem,
):
    z = lax.axis_index("gx")
    half = count * WIDE
    base = max(count, n - 1 + LAG)
    hop = (n - 1 - z, z)
    below, above = jnp.maximum(z - 1, 0), jnp.minimum(z + 1, n - 1)
    sum_to, hid_to = (below, above), (above, below)

    barrier = pltpu.get_barrier_semaphore()

    @pl.when(z > 0)
    def _():
        pl.semaphore_signal(barrier, inc=1, device_id={"gx": below}, device_id_type=MESH)

    @pl.when(z < n - 1)
    def _():
        pl.semaphore_signal(barrier, inc=1, device_id={"gx": above}, device_id_type=MESH)

    pl.semaphore_wait(barrier, jnp.minimum(z, 1) + jnp.minimum(n - 1 - z, 1))

    def weights(d, c, slot):
        columns = pl.ds(pl.multiple_of(d * half + c * WIDE, WIDE), WIDE)
        return [
            pltpu.make_async_copy(
                w.at[:, columns], wbuf.at[slot, d, :, pl.ds(i * WIDE, WIDE)], wsem.at[slot, d, i]
            )
            for i, w in enumerate((gate, up))
        ]

    def downs(d, q, slot):
        rows = pl.ds(pl.multiple_of(d * half + q * pair * WIDE, WIDE), pair * WIDE)
        return pltpu.make_async_copy(down.at[rows, :], dbuf.at[slot, d], dsem.at[slot, d])

    def sums(d, c):
        return pltpu.make_async_remote_copy(
            src_ref=part.at[d, c], dst_ref=got.at[d, c],
            send_sem=psend.at[d, lax.rem(c, 2)], recv_sem=precv.at[d, c],
            device_id={"gx": sum_to[d]}, device_id_type=MESH,
        )

    def hiddens(d, c):
        return pltpu.make_async_remote_copy(
            src_ref=hid.at[d, c], dst_ref=hid.at[d, c],
            send_sem=hsend.at[d, lax.rem(c, 2)], recv_sem=hrecv.at[d, c],
            device_id={"gx": hid_to[d]}, device_id_type=MESH,
        )

    def send(make, d, c):
        @pl.when(c >= 2)
        def _():
            make(d, c - 2).wait_send()

        make(d, c).start()

    def multiply(c):
        slot = lax.rem(c, 2)
        for d in range(2):
            for copy in weights(d, c, slot):
                copy.wait()
            part[d, c] = jnp.dot(
                tok[...], wbuf[slot, d], preferred_element_type=F32
            ).astype(BF16)

            @pl.when(c + 2 < count)
            def _():
                for copy in weights(d, c + 2, slot):
                    copy.start()

    for d in range(2):
        for c in range(min(2, count)):
            for copy in weights(d, c, c):
                copy.start()
    for d in range(2):
        for q in range(min(2, count // pair)):
            downs(d, q, q).start()
    acc[...] = jnp.zeros_like(acc)
    multiply(jnp.int32(0))

    def step(t, carry):
        for d in range(2):
            @pl.when(jnp.logical_and(hop[d] == 0, t < count))
            def _():
                send(sums, d, t)

        @pl.when(t + 1 < count)
        def _():
            multiply(t + 1)

        for d in range(2):
            c = t - hop[d]

            @pl.when(jnp.logical_and(both(1, hop[d], n - 1), both(0, c, count)))
            def _():
                sums(d, c).wait_recv()
                part[d, c] = (part[d, c].astype(F32) + got[d, c].astype(F32)).astype(BF16)
                send(sums, d, c)

        for d in range(2):
            c = t - (n - 1) - LAG

            @pl.when(jnp.logical_and(hop[d] == n - 1, both(0, c, count)))
            def _():
                sums(d, c).wait_recv()
                total = part[d, c].astype(F32) + got[d, c].astype(F32)
                g, u = total[:, :WIDE], total[:, WIDE:]
                hid[d, c] = (g / (1.0 + jnp.exp(-g)) * u).astype(BF16)

        for d in range(2):
            away = n - 1 - hop[d]
            c = t - base - away
            live = both(0, c, count)

            @pl.when(jnp.logical_and(away > 0, live))
            def _():
                hiddens(d, c).wait_recv()

            @pl.when(jnp.logical_and(away < n - 1, live))
            def _():
                send(hiddens, d, c)

        for d in range(2):
            c = t - base - (n - 1 - hop[d])
            q = c // pair

            @pl.when(jnp.logical_and(both(0, c, count), lax.rem(c, pair) == pair - 1))
            def _():
                slot = lax.rem(q, 2)
                downs(d, q, slot).wait()
                units = jnp.concatenate([hid[d, q * pair + i] for i in range(pair)], axis=1)
                acc[...] += jnp.dot(units, dbuf[slot, d], preferred_element_type=F32)

                @pl.when(q + 2 < count // pair)
                def _():
                    downs(d, q + 2, slot).start()

        return carry

    lax.fori_loop(0, base + count + n - 1, step, 0)
    out[...] = acc[...].astype(BF16)

    for d in range(2):
        for c in range(max(0, count - 2), count):
            @pl.when(hop[d] < n - 1)
            def _():
                sums(d, jnp.int32(c)).wait_send()

            @pl.when(hop[d] > 0)
            def _():
                hiddens(d, jnp.int32(c)).wait_send()


def body(n, tokens, gate_weight, up_weight, down_weight):
    features = lax.all_gather(tokens, ("gy", "gz"), axis=1, tiled=True)
    rows, depth = features.shape
    columns, width = down_weight.shape
    count = columns // (2 * WIDE)
    pair = 2 if count % 2 == 0 else 1
    projected = pl.pallas_call(
        functools.partial(kernel, n, count, pair),
        out_shape=jax.ShapeDtypeStruct((rows, width), BF16),
        in_specs=[pl.BlockSpec(memory_space=pltpu.VMEM)] + [pl.BlockSpec(memory_space=pl.ANY)] * 3,
        out_specs=pl.BlockSpec(memory_space=pltpu.VMEM),
        scratch_shapes=[
            pltpu.VMEM((2, count, rows, 2 * WIDE), BF16),
            pltpu.VMEM((2, count, rows, 2 * WIDE), BF16),
            pltpu.VMEM((2, count, rows, WIDE), BF16),
            pltpu.VMEM((rows, width), F32),
            pltpu.VMEM((2, 2, depth, 2 * WIDE), BF16),
            pltpu.VMEM((2, 2, pair * WIDE, width), BF16),
            pltpu.SemaphoreType.DMA((2, 2)),
            pltpu.SemaphoreType.DMA((2, count)),
            pltpu.SemaphoreType.DMA((2, 2)),
            pltpu.SemaphoreType.DMA((2, count)),
            pltpu.SemaphoreType.DMA((2, 2, 2)),
            pltpu.SemaphoreType.DMA((2, 2)),
        ],
        compiler_params=pltpu.CompilerParams(
            collective_id=0, has_side_effects=True, vmem_limit_bytes=60 * 2**20
        ),
    )(features, gate_weight, up_weight, down_weight)
    return lax.psum_scatter(projected, ("gy", "gz"), scatter_dimension=1, tiled=True)


def solution(mesh):
    placed = (
        P("rep", ("gx", "gy", "gz")),
        P("gx", ("gy", "gz")),
        P("gx", ("gy", "gz")),
        P(("gy", "gz"), "gx"),
    )
    return jax.shard_map(
        functools.partial(body, mesh.shape["gx"]),
        mesh=mesh, in_specs=placed, out_specs=P("rep", ("gx", "gy", "gz")), check_vma=False,
    )
```

```python
import functools

import jax
import jax.numpy as jnp
from jax import lax
from jax.experimental import pallas as pl
from jax.experimental.pallas import tpu as pltpu
from jax.sharding import PartitionSpec as P

MESH = pl.DeviceIdType.MESH
WIDE = 128
LAG = 4
FLIGHT = 4
PARTS = 2
F32, BF16 = jnp.float32, jnp.bfloat16


def both(low, value, high):
    return jnp.logical_and(value >= low, value < high)


def kernel(
    n, ny, nz, count, pair, fused, own, gate, up, down, out,
    tok, part, got, hid, acc, wbuf, dbuf, core_out, core_in, chip_out, chip_in,
    psend, precv, hsend, hrecv, wsem, dsem,
    tok_chip_send, tok_chip_recv, tok_core_send, tok_core_recv,
    core_send, core_recv, chip_send, chip_recv,
):
    z, y, k = lax.axis_index("gx"), lax.axis_index("gy"), lax.axis_index("gz")
    rows = acc.shape[0] // PARTS
    half = count * WIDE
    pairs = count // pair
    units, hunits = PARTS * count, PARTS * pairs
    ready = [(v // pairs) * count + (v % pairs + 1) * pair - 1 + n - 1 + LAG - v for v in range(hunits)]
    base = max([units] + ready)
    steps = base + hunits + n - 1
    hop = (n - 1 - z, z)
    below, above = jnp.maximum(z - 1, 0), jnp.minimum(z + 1, n - 1)
    sum_to, hid_to = (below, above), (above, below)

    barrier = pltpu.get_barrier_semaphore()

    @pl.when(z > 0)
    def _():
        pl.semaphore_signal(barrier, inc=1, device_id={"gx": below}, device_id_type=MESH)

    @pl.when(z < n - 1)
    def _():
        pl.semaphore_signal(barrier, inc=1, device_id={"gx": above}, device_id_type=MESH)

    others = 0
    if fused:
        for j in range(1, ny):
            pl.semaphore_signal(barrier, inc=1, device_id={"gy": lax.rem(y + j, ny)}, device_id_type=MESH)
        for i in range(1, nz):
            pl.semaphore_signal(barrier, inc=1, device_id={"gz": lax.rem(k + i, nz)}, device_id_type=MESH)
        others = ny + nz - 2

    def weights(d, u, slot):
        columns = pl.ds(pl.multiple_of(d * half + lax.rem(u, count) * WIDE, WIDE), WIDE)
        return [
            pltpu.make_async_copy(
                w.at[:, columns], wbuf.at[slot, d, :, pl.ds(i * WIDE, WIDE)], wsem.at[slot, d, i]
            )
            for i, w in enumerate((gate, up))
        ]

    def downs(d, v, slot):
        q = lax.rem(v, pairs)
        units_of = pl.ds(pl.multiple_of(d * half + q * pair * WIDE, WIDE), pair * WIDE)
        return pltpu.make_async_copy(down.at[units_of, :], dbuf.at[slot, d], dsem.at[slot, d])

    def sums(d, u):
        return pltpu.make_async_remote_copy(
            src_ref=part.at[d, u], dst_ref=got.at[d, u],
            send_sem=psend.at[d, lax.rem(u, FLIGHT)], recv_sem=precv.at[d, u],
            device_id={"gx": sum_to[d]}, device_id_type=MESH,
        )

    def hiddens(d, v):
        block = hid.at[d, pl.ds(v * pair, pair)]
        return pltpu.make_async_remote_copy(
            src_ref=block, dst_ref=block,
            send_sem=hsend.at[d, lax.rem(v, FLIGHT)], recv_sem=hrecv.at[d, v],
            device_id={"gx": hid_to[d]}, device_id_type=MESH,
        )

    def send(make, d, u):
        @pl.when(u >= FLIGHT)
        def _():
            make(d, u - FLIGHT).wait_send()

        make(d, u).start()

    def rows_of(r):
        return pl.ds(r * rows, rows)

    def block_of(yy, kk):
        width = own.shape[1]
        return pl.ds(pl.multiple_of((yy * nz + kk) * width, WIDE), width)

    def tok_chip(r, j):
        return pltpu.make_async_remote_copy(
            src_ref=own.at[rows_of(r), :], dst_ref=tok.at[rows_of(r), block_of(y, k)],
            send_sem=tok_chip_send.at[r, j], recv_sem=tok_chip_recv.at[r, j],
            device_id={"gy": lax.rem(y + j, ny)}, device_id_type=MESH,
        )

    def tok_core(r, i, j):
        block = tok.at[rows_of(r), block_of(lax.rem(y + ny - j, ny), k)]
        return pltpu.make_async_remote_copy(
            src_ref=own.at[rows_of(r), :] if j == 0 else block, dst_ref=block,
            send_sem=tok_core_send.at[r, i, j], recv_sem=tok_core_recv.at[r, i, j],
            device_id={"gz": lax.rem(k + i, nz)}, device_id_type=MESH,
        )

    def tok_start():
        for r in range(PARTS):
            for j in range(1, ny):
                tok_chip(r, j).start()
        for r in range(PARTS):
            for i in range(1, nz):
                tok_core(r, i, 0).start()
        tok[:, block_of(y, k)] = own[...]

    def tok_hand_on(r):
        for j in range(1, ny):
            tok_chip(r, j).wait_recv()
            for i in range(1, nz):
                tok_core(r, i, j).start()

    def tok_finish(r):
        for i in range(1, nz):
            for j in range(ny):
                tok_core(r, i, j).wait_recv()
        for j in range(1, ny):
            tok_chip(r, j).wait_send()
        for i in range(1, nz):
            for j in range(ny):
                tok_core(r, i, j).wait_send()

    def out_block(yy, kk):
        width = out.shape[1]
        return pl.ds(pl.multiple_of((yy * nz + kk) * width, WIDE), width)

    def core_copy(r, i):
        return pltpu.make_async_remote_copy(
            src_ref=core_out.at[r, i - 1], dst_ref=core_in.at[r, i - 1],
            send_sem=core_send.at[r, i], recv_sem=core_recv.at[r, i],
            device_id={"gz": lax.rem(k + i, nz)}, device_id_type=MESH,
        )

    def chip_copy(r, j):
        return pltpu.make_async_remote_copy(
            src_ref=chip_out.at[r, j - 1], dst_ref=chip_in.at[r, j - 1],
            send_sem=chip_send.at[r, j], recv_sem=chip_recv.at[r, j],
            device_id={"gy": lax.rem(y + j, ny)}, device_id_type=MESH,
        )

    def out_cores(r):
        for i in range(1, nz):
            for yy in range(ny):
                core_out[r, i - 1, yy] = acc[rows_of(r), out_block(yy, lax.rem(k + i, nz))].astype(BF16)
            core_copy(r, i).start()

    def chip_sum(r, yy):
        total = acc[rows_of(r), out_block(yy, k)]
        for i in range(1, nz):
            total += core_in[r, i - 1, yy].astype(F32)
        return total

    def out_chips(r):
        for i in range(1, nz):
            core_copy(r, i).wait()
        for j in range(1, ny):
            chip_out[r, j - 1] = chip_sum(r, lax.rem(y + j, ny)).astype(BF16)
            chip_copy(r, j).start()

    def out_finish(r):
        total = chip_sum(r, y)
        for j in range(1, ny):
            chip_copy(r, j).wait()
            total += chip_in[r, j - 1].astype(F32)
        out[rows_of(r), :] = total.astype(BF16)

    features = tok if fused else own

    def multiply(u):
        slot = lax.rem(u, 2)
        first = pl.multiple_of((u // count) * rows, rows)
        for d in range(2):
            for copy in weights(d, u, slot):
                copy.wait()
            part[d, u] = jnp.dot(
                features[pl.ds(first, rows), :], wbuf[slot, d], preferred_element_type=F32
            ).astype(BF16)

            @pl.when(u + 2 < units)
            def _():
                for copy in weights(d, u + 2, slot):
                    copy.start()

    for c in range(2):
        for d in range(2):
            for copy in weights(d, jnp.int32(c), c):
                copy.start()
    for d in range(2):
        for v in range(2):
            downs(d, jnp.int32(v), v).start()
    pl.semaphore_wait(barrier, jnp.minimum(z, 1) + jnp.minimum(n - 1 - z, 1) + others)
    if fused:
        tok_start()
        acc[...] = jnp.zeros_like(acc)
        tok_hand_on(0)
        tok_finish(0)
    else:
        acc[...] = jnp.zeros_like(acc)
    multiply(jnp.int32(0))

    def step(t, carry):
        for d in range(2):
            @pl.when(jnp.logical_and(hop[d] == 0, t < units))
            def _():
                send(sums, d, t)

        if fused:
            for r in range(1, PARTS):
                @pl.when(t == min(4, count - 2))
                def _():
                    tok_hand_on(r)

                @pl.when(t == min(8, count - 2))
                def _():
                    tok_finish(r)

        @pl.when(t + 1 < units)
        def _():
            multiply(t + 1)

        for d in range(2):
            u = t - hop[d]

            @pl.when(jnp.logical_and(both(1, hop[d], n - 1), both(0, u, units)))
            def _():
                sums(d, u).wait_recv()
                part[d, u] = (part[d, u].astype(F32) + got[d, u].astype(F32)).astype(BF16)
                send(sums, d, u)

        for d in range(2):
            u = t - (n - 1) - LAG

            @pl.when(jnp.logical_and(hop[d] == n - 1, both(0, u, units)))
            def _():
                sums(d, u).wait_recv()
                total = part[d, u].astype(F32) + got[d, u].astype(F32)
                g, w = total[:, :WIDE], total[:, WIDE:]
                hid[d, u] = (g / (1.0 + jnp.exp(-g)) * w).astype(BF16)

        for d in range(2):
            away = n - 1 - hop[d]
            v = t - base - away
            live = both(0, v, hunits)

            @pl.when(jnp.logical_and(away > 0, live))
            def _():
                hiddens(d, v).wait_recv()

            @pl.when(jnp.logical_and(away < n - 1, live))
            def _():
                send(hiddens, d, v)

            @pl.when(live)
            def _():
                slot = lax.rem(v, 2)
                downs(d, v, slot).wait()
                first = pl.ds(pl.multiple_of((v // pairs) * rows, rows), rows)
                block = jnp.concatenate([hid[d, v * pair + i] for i in range(pair)], axis=1)
                acc[first, :] += jnp.dot(block, dbuf[slot, d], preferred_element_type=F32)

                @pl.when(v + 2 < hunits)
                def _():
                    downs(d, v + 2, slot).start()

        if fused:
            for r in range(PARTS - 1):
                whole = base + (r + 1) * pairs - 1 + n - 1
                for stage, after in ((out_cores, 0), (out_chips, 2), (out_finish, 6)):
                    @pl.when(t == min(whole + after, steps - 1))
                    def _():
                        stage(r)

        return carry

    lax.fori_loop(0, steps, step, 0)
    if fused:
        for stage in (out_cores, out_chips, out_finish):
            stage(PARTS - 1)
    else:
        out[...] = acc[...].astype(BF16)

    for d in range(2):
        @pl.when(hop[d] < n - 1)
        def _():
            for u in range(units - FLIGHT, units):
                sums(d, jnp.int32(u)).wait_send()

        @pl.when(hop[d] > 0)
        def _():
            for v in range(hunits - FLIGHT, hunits):
                hiddens(d, jnp.int32(v)).wait_send()


def body(n, ny, nz, tokens, gate_weight, up_weight, down_weight):
    depth = gate_weight.shape[0]
    columns, width = down_weight.shape
    fused = tokens.shape[1] % WIDE == 0 and width % (ny * nz * WIDE) == 0
    if not fused:
        tokens = lax.all_gather(tokens, ("gy", "gz"), axis=1, tiled=True)
    rows = tokens.shape[0]
    own_width = width // (ny * nz) if fused else width
    count = columns // (2 * WIDE)
    pair = 2 if count % 2 == 0 else 1
    units, part_rows = PARTS * count, rows // PARTS
    dma = pltpu.SemaphoreType.DMA
    result = pl.pallas_call(
        functools.partial(kernel, n, ny, nz, count, pair, fused),
        out_shape=jax.ShapeDtypeStruct((rows, own_width), BF16),
        in_specs=[pl.BlockSpec(memory_space=pltpu.VMEM)] + [pl.BlockSpec(memory_space=pl.ANY)] * 3,
        out_specs=pl.BlockSpec(memory_space=pltpu.VMEM),
        scratch_shapes=[
            pltpu.VMEM((rows, depth) if fused else (16, WIDE), BF16),
            pltpu.VMEM((2, units, part_rows, 2 * WIDE), BF16),
            pltpu.VMEM((2, units, part_rows, 2 * WIDE), BF16),
            pltpu.VMEM((2, units, part_rows, WIDE), BF16),
            pltpu.VMEM((rows, width), F32),
            pltpu.VMEM((2, 2, depth, 2 * WIDE), BF16),
            pltpu.VMEM((2, 2, pair * WIDE, width), BF16),
            *[
                pltpu.VMEM(shape if fused else (16, WIDE), BF16)
                for shape in [(PARTS, nz - 1, ny, part_rows, own_width)] * 2
                + [(PARTS, ny - 1, part_rows, own_width)] * 2
            ],
            dma((2, FLIGHT)), dma((2, units)), dma((2, FLIGHT)), dma((2, units // pair)),
            dma((2, 2, 2)), dma((2, 2)),
            dma((PARTS, ny)), dma((PARTS, ny)), dma((PARTS, nz, ny)), dma((PARTS, nz, ny)),
            dma((PARTS, nz)), dma((PARTS, nz)), dma((PARTS, ny)), dma((PARTS, ny)),
        ],
        compiler_params=pltpu.CompilerParams(
            collective_id=0, has_side_effects=True, vmem_limit_bytes=60 * 2**20
        ),
    )(tokens, gate_weight, up_weight, down_weight)
    if fused:
        return result
    return lax.psum_scatter(result, ("gy", "gz"), scatter_dimension=1, tiled=True)


def solution(mesh):
    placed = (
        P("rep", ("gx", "gy", "gz")),
        P("gx", ("gy", "gz")),
        P("gx", ("gy", "gz")),
        P(("gy", "gz"), "gx"),
    )
    return jax.shard_map(
        functools.partial(body, mesh.shape["gx"], mesh.shape["gy"], mesh.shape["gz"]),
        mesh=mesh, in_specs=placed, out_specs=P("rep", ("gx", "gy", "gz")), check_vma=False,
    )
```

```python
import functools

import jax
import jax.numpy as jnp
from jax import lax
from jax.experimental import pallas as pl
from jax.experimental.pallas import tpu as pltpu
from jax.sharding import PartitionSpec as P

MESH = pl.DeviceIdType.MESH
WIDE = 128
LAG = 2
SPACE = 3
FLIGHT = 4
PARTS = 2
F32, BF16 = jnp.float32, jnp.bfloat16


def both(low, value, high):
    return jnp.logical_and(value >= low, value < high)


def kernel(
    n, ny, nz, count, pair, fused, own, gate, up, down, out,
    tok, part, got, hid, acc, wbuf, dbuf, core_out, core_in, chip_out, chip_in,
    psend, precv, hsend, hrecv, wsem, dsem,
    tok_chip_send, tok_chip_recv, tok_core_send, tok_core_recv,
    core_send, core_recv, chip_send, chip_recv,
):
    z, y, k = lax.axis_index("gx"), lax.axis_index("gy"), lax.axis_index("gz")
    rows = acc.shape[0] // PARTS
    half = count * WIDE
    pairs = count // pair
    units, hunits = PARTS * count, PARTS * pairs
    ready = [(v // pairs) * count + (v % pairs + 1) * pair - 1 + SPACE * (n - 1) + LAG - v for v in range(hunits)]
    base = max([units] + ready)
    steps = base + hunits + SPACE * (n - 1)
    hop = (n - 1 - z, z)
    below, above = jnp.maximum(z - 1, 0), jnp.minimum(z + 1, n - 1)
    sum_to, hid_to = (below, above), (above, below)

    barrier = pltpu.get_barrier_semaphore()

    @pl.when(z > 0)
    def _():
        pl.semaphore_signal(barrier, inc=1, device_id={"gx": below}, device_id_type=MESH)

    @pl.when(z < n - 1)
    def _():
        pl.semaphore_signal(barrier, inc=1, device_id={"gx": above}, device_id_type=MESH)

    others = 0
    if fused:
        for j in range(1, ny):
            pl.semaphore_signal(barrier, inc=1, device_id={"gy": lax.rem(y + j, ny)}, device_id_type=MESH)
        for i in range(1, nz):
            pl.semaphore_signal(barrier, inc=1, device_id={"gz": lax.rem(k + i, nz)}, device_id_type=MESH)
        others = ny + nz - 2

    def weights(d, u, slot):
        columns = pl.ds(pl.multiple_of(d * half + lax.rem(u, count) * WIDE, WIDE), WIDE)
        return [
            pltpu.make_async_copy(
                w.at[:, columns], wbuf.at[slot, d, :, pl.ds(i * WIDE, WIDE)], wsem.at[slot, d, i]
            )
            for i, w in enumerate((gate, up))
        ]

    def downs(d, v, slot):
        q = lax.rem(v, pairs)
        units_of = pl.ds(pl.multiple_of(d * half + q * pair * WIDE, WIDE), pair * WIDE)
        return pltpu.make_async_copy(down.at[units_of, :], dbuf.at[slot, d], dsem.at[slot, d])

    def sums(d, u):
        return pltpu.make_async_remote_copy(
            src_ref=part.at[d, u], dst_ref=got.at[d, u],
            send_sem=psend.at[d, lax.rem(u, FLIGHT)], recv_sem=precv.at[d, u],
            device_id={"gx": sum_to[d]}, device_id_type=MESH,
        )

    def hiddens(d, v):
        block = hid.at[d, pl.ds(v * pair, pair)]
        return pltpu.make_async_remote_copy(
            src_ref=block, dst_ref=block,
            send_sem=hsend.at[d, lax.rem(v, FLIGHT)], recv_sem=hrecv.at[d, v],
            device_id={"gx": hid_to[d]}, device_id_type=MESH,
        )

    def send(make, d, u):
        @pl.when(u >= FLIGHT)
        def _():
            make(d, u - FLIGHT).wait_send()

        make(d, u).start()

    def rows_of(r):
        return pl.ds(r * rows, rows)

    def block_of(yy, kk):
        width = own.shape[1]
        return pl.ds(pl.multiple_of((yy * nz + kk) * width, WIDE), width)

    def tok_chip(r, j):
        return pltpu.make_async_remote_copy(
            src_ref=own.at[rows_of(r), :], dst_ref=tok.at[rows_of(r), block_of(y, k)],
            send_sem=tok_chip_send.at[r, j], recv_sem=tok_chip_recv.at[r, j],
            device_id={"gy": lax.rem(y + j, ny)}, device_id_type=MESH,
        )

    def tok_core(r, i, j):
        block = tok.at[rows_of(r), block_of(lax.rem(y + ny - j, ny), k)]
        return pltpu.make_async_remote_copy(
            src_ref=own.at[rows_of(r), :] if j == 0 else block, dst_ref=block,
            send_sem=tok_core_send.at[r, i, j], recv_sem=tok_core_recv.at[r, i, j],
            device_id={"gz": lax.rem(k + i, nz)}, device_id_type=MESH,
        )

    def tok_start():
        for r in range(PARTS):
            for j in range(1, ny):
                tok_chip(r, j).start()
        for r in range(PARTS):
            for i in range(1, nz):
                tok_core(r, i, 0).start()
        tok[:, block_of(y, k)] = own[...]

    def tok_hand_on(r):
        for j in range(1, ny):
            tok_chip(r, j).wait_recv()
            for i in range(1, nz):
                tok_core(r, i, j).start()

    def tok_finish(r):
        for i in range(1, nz):
            for j in range(ny):
                tok_core(r, i, j).wait_recv()
        for j in range(1, ny):
            tok_chip(r, j).wait_send()
        for i in range(1, nz):
            for j in range(ny):
                tok_core(r, i, j).wait_send()

    def out_block(yy, kk):
        width = out.shape[1]
        return pl.ds(pl.multiple_of((yy * nz + kk) * width, WIDE), width)

    def core_copy(r, i):
        return pltpu.make_async_remote_copy(
            src_ref=core_out.at[r, i - 1], dst_ref=core_in.at[r, i - 1],
            send_sem=core_send.at[r, i], recv_sem=core_recv.at[r, i],
            device_id={"gz": lax.rem(k + i, nz)}, device_id_type=MESH,
        )

    def chip_copy(r, j):
        return pltpu.make_async_remote_copy(
            src_ref=chip_out.at[r, j - 1], dst_ref=chip_in.at[r, j - 1],
            send_sem=chip_send.at[r, j], recv_sem=chip_recv.at[r, j],
            device_id={"gy": lax.rem(y + j, ny)}, device_id_type=MESH,
        )

    def out_cores(r):
        for i in range(1, nz):
            for yy in range(ny):
                core_out[r, i - 1, yy] = acc[rows_of(r), out_block(yy, lax.rem(k + i, nz))].astype(BF16)
            core_copy(r, i).start()

    def chip_sum(r, yy):
        total = acc[rows_of(r), out_block(yy, k)]
        for i in range(1, nz):
            total += core_in[r, i - 1, yy].astype(F32)
        return total

    def out_chips(r):
        for i in range(1, nz):
            core_copy(r, i).wait()
        for j in range(1, ny):
            chip_out[r, j - 1] = chip_sum(r, lax.rem(y + j, ny)).astype(BF16)
            chip_copy(r, j).start()

    def out_finish(r):
        total = chip_sum(r, y)
        for j in range(1, ny):
            chip_copy(r, j).wait()
            total += chip_in[r, j - 1].astype(F32)
        out[rows_of(r), :] = total.astype(BF16)

    features = tok if fused else own

    def multiply(u):
        slot = lax.rem(u, 2)
        first = pl.multiple_of((u // count) * rows, rows)
        for d in range(2):
            for copy in weights(d, u, slot):
                copy.wait()
            part[d, u] = jnp.dot(
                features[pl.ds(first, rows), :], wbuf[slot, d], preferred_element_type=F32
            ).astype(BF16)

            @pl.when(u + 2 < units)
            def _():
                for copy in weights(d, u + 2, slot):
                    copy.start()

    for c in range(2):
        for d in range(2):
            for copy in weights(d, jnp.int32(c), c):
                copy.start()
    for d in range(2):
        for v in range(2):
            downs(d, jnp.int32(v), v).start()
    pl.semaphore_wait(barrier, jnp.minimum(z, 1) + jnp.minimum(n - 1 - z, 1) + others)
    if fused:
        tok_start()
        acc[...] = jnp.zeros_like(acc)
        tok_hand_on(0)
        tok_finish(0)
    else:
        acc[...] = jnp.zeros_like(acc)
    multiply(jnp.int32(0))

    def step(t, carry):
        for d in range(2):
            @pl.when(jnp.logical_and(hop[d] == 0, t < units))
            def _():
                send(sums, d, t)

        if fused:
            for r in range(1, PARTS):
                @pl.when(t == min(4, count - 2))
                def _():
                    tok_hand_on(r)

                @pl.when(t == min(8, count - 2))
                def _():
                    tok_finish(r)

        @pl.when(t + 1 < units)
        def _():
            multiply(t + 1)

        for d in range(2):
            u = t - SPACE * hop[d]

            @pl.when(jnp.logical_and(both(1, hop[d], n - 1), both(0, u, units)))
            def _():
                sums(d, u).wait_recv()
                part[d, u] = (part[d, u].astype(F32) + got[d, u].astype(F32)).astype(BF16)
                send(sums, d, u)

        for d in range(2):
            u = t - SPACE * (n - 1) - LAG

            @pl.when(jnp.logical_and(hop[d] == n - 1, both(0, u, units)))
            def _():
                sums(d, u).wait_recv()
                total = part[d, u].astype(F32) + got[d, u].astype(F32)
                g, w = total[:, :WIDE], total[:, WIDE:]
                hid[d, u] = (g / (1.0 + jnp.exp(-g)) * w).astype(BF16)

        for d in range(2):
            away = n - 1 - hop[d]
            v = t - base - SPACE * away
            live = both(0, v, hunits)

            @pl.when(jnp.logical_and(away > 0, live))
            def _():
                hiddens(d, v).wait_recv()

            @pl.when(jnp.logical_and(away < n - 1, live))
            def _():
                send(hiddens, d, v)

            @pl.when(live)
            def _():
                slot = lax.rem(v, 2)
                downs(d, v, slot).wait()
                first = pl.ds(pl.multiple_of((v // pairs) * rows, rows), rows)
                block = jnp.concatenate([hid[d, v * pair + i] for i in range(pair)], axis=1)
                acc[first, :] += jnp.dot(block, dbuf[slot, d], preferred_element_type=F32)

                @pl.when(v + 2 < hunits)
                def _():
                    downs(d, v + 2, slot).start()

        if fused:
            for r in range(PARTS - 1):
                whole = base + (r + 1) * pairs - 1 + SPACE * (n - 1)
                for stage, after in ((out_cores, 0), (out_chips, 2), (out_finish, 6)):
                    @pl.when(t == min(whole + after, steps - 1))
                    def _():
                        stage(r)

        return carry

    lax.fori_loop(0, steps, step, 0)
    if fused:
        for stage in (out_cores, out_chips, out_finish):
            stage(PARTS - 1)
    else:
        out[...] = acc[...].astype(BF16)

    for d in range(2):
        @pl.when(hop[d] < n - 1)
        def _():
            for u in range(units - FLIGHT, units):
                sums(d, jnp.int32(u)).wait_send()

        @pl.when(hop[d] > 0)
        def _():
            for v in range(hunits - FLIGHT, hunits):
                hiddens(d, jnp.int32(v)).wait_send()


def body(n, ny, nz, tokens, gate_weight, up_weight, down_weight):
    depth = gate_weight.shape[0]
    columns, width = down_weight.shape
    fused = tokens.shape[1] % WIDE == 0 and width % (ny * nz * WIDE) == 0
    if not fused:
        tokens = lax.all_gather(tokens, ("gy", "gz"), axis=1, tiled=True)
    rows = tokens.shape[0]
    own_width = width // (ny * nz) if fused else width
    count = columns // (2 * WIDE)
    pair = 2 if count % 2 == 0 else 1
    units, part_rows = PARTS * count, rows // PARTS
    dma = pltpu.SemaphoreType.DMA
    result = pl.pallas_call(
        functools.partial(kernel, n, ny, nz, count, pair, fused),
        out_shape=jax.ShapeDtypeStruct((rows, own_width), BF16),
        in_specs=[pl.BlockSpec(memory_space=pltpu.VMEM)] + [pl.BlockSpec(memory_space=pl.ANY)] * 3,
        out_specs=pl.BlockSpec(memory_space=pltpu.VMEM),
        scratch_shapes=[
            pltpu.VMEM((rows, depth) if fused else (16, WIDE), BF16),
            pltpu.VMEM((2, units, part_rows, 2 * WIDE), BF16),
            pltpu.VMEM((2, units, part_rows, 2 * WIDE), BF16),
            pltpu.VMEM((2, units, part_rows, WIDE), BF16),
            pltpu.VMEM((rows, width), F32),
            pltpu.VMEM((2, 2, depth, 2 * WIDE), BF16),
            pltpu.VMEM((2, 2, pair * WIDE, width), BF16),
            *[
                pltpu.VMEM(shape if fused else (16, WIDE), BF16)
                for shape in [(PARTS, nz - 1, ny, part_rows, own_width)] * 2
                + [(PARTS, ny - 1, part_rows, own_width)] * 2
            ],
            dma((2, FLIGHT)), dma((2, units)), dma((2, FLIGHT)), dma((2, units // pair)),
            dma((2, 2, 2)), dma((2, 2)),
            dma((PARTS, ny)), dma((PARTS, ny)), dma((PARTS, nz, ny)), dma((PARTS, nz, ny)),
            dma((PARTS, nz)), dma((PARTS, nz)), dma((PARTS, ny)), dma((PARTS, ny)),
        ],
        compiler_params=pltpu.CompilerParams(
            collective_id=0, has_side_effects=True, vmem_limit_bytes=60 * 2**20
        ),
    )(tokens, gate_weight, up_weight, down_weight)
    if fused:
        return result
    return lax.psum_scatter(result, ("gy", "gz"), scatter_dimension=1, tiled=True)


def solution(mesh):
    placed = (
        P("rep", ("gx", "gy", "gz")),
        P("gx", ("gy", "gz")),
        P("gx", ("gy", "gz")),
        P(("gy", "gz"), "gx"),
    )
    return jax.shard_map(
        functools.partial(body, mesh.shape["gx"], mesh.shape["gy"], mesh.shape["gz"]),
        mesh=mesh, in_specs=placed, out_specs=P("rep", ("gx", "gy", "gz")), check_vma=False,
    )
```

```python
import functools

import jax
import jax.numpy as jnp
from jax import lax
from jax.experimental import pallas as pl
from jax.experimental.pallas import tpu as pltpu
from jax.sharding import PartitionSpec as P

MESH = pl.DeviceIdType.MESH
WIDE = 128
LAG = 2
SPACE = 2
FLIGHT = 4
PARTS = 2
F32, BF16 = jnp.float32, jnp.bfloat16


def both(low, value, high):
    return jnp.logical_and(value >= low, value < high)


def kernel(
    n, ny, nz, count, pair, fused, own, gate, up, down, out,
    tok, part, got, hid, acc, wbuf, dbuf, core_out, core_in, chip_out, chip_in,
    psend, precv, hsend, hrecv, wsem, dsem,
    tok_chip_send, tok_chip_recv, tok_core_send, tok_core_recv,
    core_send, core_recv, chip_send, chip_recv,
):
    z, y, k = lax.axis_index("gx"), lax.axis_index("gy"), lax.axis_index("gz")
    rows = acc.shape[0] // PARTS
    half = count * WIDE
    pairs = count // pair
    units, hunits = PARTS * count, PARTS * pairs
    ready = [(v // pairs) * count + (v % pairs + 1) * pair - 1 + SPACE * (n - 1) + LAG - v for v in range(hunits)]
    base = max([units] + ready)
    steps = base + hunits + SPACE * (n - 1)
    hop = (n - 1 - z, z)
    below, above = jnp.maximum(z - 1, 0), jnp.minimum(z + 1, n - 1)
    sum_to, hid_to = (below, above), (above, below)

    barrier = pltpu.get_barrier_semaphore()

    @pl.when(z > 0)
    def _():
        pl.semaphore_signal(barrier, inc=1, device_id={"gx": below}, device_id_type=MESH)

    @pl.when(z < n - 1)
    def _():
        pl.semaphore_signal(barrier, inc=1, device_id={"gx": above}, device_id_type=MESH)

    others = 0
    if fused:
        for j in range(1, ny):
            pl.semaphore_signal(barrier, inc=1, device_id={"gy": lax.rem(y + j, ny)}, device_id_type=MESH)
        for i in range(1, nz):
            pl.semaphore_signal(barrier, inc=1, device_id={"gz": lax.rem(k + i, nz)}, device_id_type=MESH)
        others = ny + nz - 2

    def weights(d, u, slot):
        columns = pl.ds(pl.multiple_of(d * half + lax.rem(u, count) * WIDE, WIDE), WIDE)
        return [
            pltpu.make_async_copy(
                w.at[:, columns], wbuf.at[slot, d, :, pl.ds(i * WIDE, WIDE)], wsem.at[slot, d, i]
            )
            for i, w in enumerate((gate, up))
        ]

    def downs(d, v, slot):
        q = lax.rem(v, pairs)
        units_of = pl.ds(pl.multiple_of(d * half + q * pair * WIDE, WIDE), pair * WIDE)
        return pltpu.make_async_copy(down.at[units_of, :], dbuf.at[slot, d], dsem.at[slot, d])

    def sums(d, u):
        return pltpu.make_async_remote_copy(
            src_ref=part.at[d, u], dst_ref=got.at[d, u],
            send_sem=psend.at[d, lax.rem(u, FLIGHT)], recv_sem=precv.at[d, u],
            device_id={"gx": sum_to[d]}, device_id_type=MESH,
        )

    def hiddens(d, v):
        block = hid.at[d, pl.ds(v * pair, pair)]
        return pltpu.make_async_remote_copy(
            src_ref=block, dst_ref=block,
            send_sem=hsend.at[d, lax.rem(v, FLIGHT)], recv_sem=hrecv.at[d, v],
            device_id={"gx": hid_to[d]}, device_id_type=MESH,
        )

    def send(make, d, u):
        @pl.when(u >= FLIGHT)
        def _():
            make(d, u - FLIGHT).wait_send()

        make(d, u).start()

    def rows_of(r):
        return pl.ds(r * rows, rows)

    def block_of(yy, kk):
        width = own.shape[1]
        return pl.ds(pl.multiple_of((yy * nz + kk) * width, WIDE), width)

    def tok_chip(r, j):
        return pltpu.make_async_remote_copy(
            src_ref=own.at[rows_of(r), :], dst_ref=tok.at[rows_of(r), block_of(y, k)],
            send_sem=tok_chip_send.at[r, j], recv_sem=tok_chip_recv.at[r, j],
            device_id={"gy": lax.rem(y + j, ny)}, device_id_type=MESH,
        )

    def tok_core(r, i, j):
        block = tok.at[rows_of(r), block_of(lax.rem(y + ny - j, ny), k)]
        return pltpu.make_async_remote_copy(
            src_ref=own.at[rows_of(r), :] if j == 0 else block, dst_ref=block,
            send_sem=tok_core_send.at[r, i, j], recv_sem=tok_core_recv.at[r, i, j],
            device_id={"gz": lax.rem(k + i, nz)}, device_id_type=MESH,
        )

    def tok_start():
        for r in range(PARTS):
            for j in range(1, ny):
                tok_chip(r, j).start()
        for r in range(PARTS):
            for i in range(1, nz):
                tok_core(r, i, 0).start()
        tok[:, block_of(y, k)] = own[...]

    def tok_hand_on(r):
        for j in range(1, ny):
            tok_chip(r, j).wait_recv()
            for i in range(1, nz):
                tok_core(r, i, j).start()

    def tok_finish(r):
        for i in range(1, nz):
            for j in range(ny):
                tok_core(r, i, j).wait_recv()
        for j in range(1, ny):
            tok_chip(r, j).wait_send()
        for i in range(1, nz):
            for j in range(ny):
                tok_core(r, i, j).wait_send()

    def out_block(yy, kk):
        width = out.shape[1]
        return pl.ds(pl.multiple_of((yy * nz + kk) * width, WIDE), width)

    def core_copy(r, i):
        return pltpu.make_async_remote_copy(
            src_ref=core_out.at[r, i - 1], dst_ref=core_in.at[r, i - 1],
            send_sem=core_send.at[r, i], recv_sem=core_recv.at[r, i],
            device_id={"gz": lax.rem(k + i, nz)}, device_id_type=MESH,
        )

    def chip_copy(r, j):
        return pltpu.make_async_remote_copy(
            src_ref=chip_out.at[r, j - 1], dst_ref=chip_in.at[r, j - 1],
            send_sem=chip_send.at[r, j], recv_sem=chip_recv.at[r, j],
            device_id={"gy": lax.rem(y + j, ny)}, device_id_type=MESH,
        )

    def out_cores(r):
        for i in range(1, nz):
            for yy in range(ny):
                core_out[r, i - 1, yy] = acc[rows_of(r), out_block(yy, lax.rem(k + i, nz))].astype(BF16)
            core_copy(r, i).start()

    def chip_sum(r, yy):
        total = acc[rows_of(r), out_block(yy, k)]
        for i in range(1, nz):
            total += core_in[r, i - 1, yy].astype(F32)
        return total

    def out_chips(r):
        for i in range(1, nz):
            core_copy(r, i).wait()
        for j in range(1, ny):
            chip_out[r, j - 1] = chip_sum(r, lax.rem(y + j, ny)).astype(BF16)
            chip_copy(r, j).start()

    def out_finish(r):
        total = chip_sum(r, y)
        for j in range(1, ny):
            chip_copy(r, j).wait()
            total += chip_in[r, j - 1].astype(F32)
        out[rows_of(r), :] = total.astype(BF16)

    features = tok if fused else own

    def multiply(u):
        slot = lax.rem(u, 2)
        first = pl.multiple_of((u // count) * rows, rows)
        for d in range(2):
            for copy in weights(d, u, slot):
                copy.wait()
            part[d, u] = jnp.dot(
                features[pl.ds(first, rows), :], wbuf[slot, d], preferred_element_type=F32
            ).astype(BF16)

            @pl.when(u + 2 < units)
            def _():
                for copy in weights(d, u + 2, slot):
                    copy.start()

    for c in range(2):
        for d in range(2):
            for copy in weights(d, jnp.int32(c), c):
                copy.start()
    for d in range(2):
        for v in range(2):
            downs(d, jnp.int32(v), v).start()
    pl.semaphore_wait(barrier, jnp.minimum(z, 1) + jnp.minimum(n - 1 - z, 1) + others)
    if fused:
        tok_start()
        acc[...] = jnp.zeros_like(acc)
        tok_hand_on(0)
        tok_finish(0)
    else:
        acc[...] = jnp.zeros_like(acc)
    multiply(jnp.int32(0))

    def step(t, carry):
        for d in range(2):
            @pl.when(jnp.logical_and(hop[d] == 0, t < units))
            def _():
                send(sums, d, t)

        if fused:
            for r in range(1, PARTS):
                @pl.when(t == min(4, count - 2))
                def _():
                    tok_hand_on(r)

                @pl.when(t == min(8, count - 2))
                def _():
                    tok_finish(r)

        @pl.when(t + 1 < units)
        def _():
            multiply(t + 1)

        for d in range(2):
            u = t - SPACE * hop[d]

            @pl.when(jnp.logical_and(both(1, hop[d], n - 1), both(0, u, units)))
            def _():
                sums(d, u).wait_recv()
                part[d, u] = (part[d, u].astype(F32) + got[d, u].astype(F32)).astype(BF16)
                send(sums, d, u)

        for d in range(2):
            u = t - SPACE * (n - 1) - LAG

            @pl.when(jnp.logical_and(hop[d] == n - 1, both(0, u, units)))
            def _():
                sums(d, u).wait_recv()
                total = part[d, u].astype(F32) + got[d, u].astype(F32)
                g, w = total[:, :WIDE], total[:, WIDE:]
                hid[d, u] = (g / (1.0 + jnp.exp(-g)) * w).astype(BF16)

        for d in range(2):
            away = n - 1 - hop[d]
            v = t - base - SPACE * away
            live = both(0, v, hunits)

            @pl.when(jnp.logical_and(away > 0, live))
            def _():
                hiddens(d, v).wait_recv()

            @pl.when(jnp.logical_and(away < n - 1, live))
            def _():
                send(hiddens, d, v)

            @pl.when(live)
            def _():
                slot = lax.rem(v, 2)
                downs(d, v, slot).wait()
                first = pl.ds(pl.multiple_of((v // pairs) * rows, rows), rows)
                block = jnp.concatenate([hid[d, v * pair + i] for i in range(pair)], axis=1)
                acc[first, :] += jnp.dot(block, dbuf[slot, d], preferred_element_type=F32)

                @pl.when(v + 2 < hunits)
                def _():
                    downs(d, v + 2, slot).start()

        if fused:
            for r in range(PARTS - 1):
                whole = base + (r + 1) * pairs - 1 + SPACE * (n - 1)
                for stage, after in ((out_cores, 0), (out_chips, 2), (out_finish, 6)):
                    @pl.when(t == min(whole + after, steps - 1))
                    def _():
                        stage(r)

        return carry

    lax.fori_loop(0, steps, step, 0)
    if fused:
        for stage in (out_cores, out_chips, out_finish):
            stage(PARTS - 1)
    else:
        out[...] = acc[...].astype(BF16)

    for d in range(2):
        @pl.when(hop[d] < n - 1)
        def _():
            for u in range(units - FLIGHT, units):
                sums(d, jnp.int32(u)).wait_send()

        @pl.when(hop[d] > 0)
        def _():
            for v in range(hunits - FLIGHT, hunits):
                hiddens(d, jnp.int32(v)).wait_send()


def body(n, ny, nz, tokens, gate_weight, up_weight, down_weight):
    depth = gate_weight.shape[0]
    columns, width = down_weight.shape
    fused = tokens.shape[1] % WIDE == 0 and width % (ny * nz * WIDE) == 0
    if not fused:
        tokens = lax.all_gather(tokens, ("gy", "gz"), axis=1, tiled=True)
    rows = tokens.shape[0]
    own_width = width // (ny * nz) if fused else width
    count = columns // (2 * WIDE)
    pair = 2 if count % 2 == 0 else 1
    units, part_rows = PARTS * count, rows // PARTS
    dma = pltpu.SemaphoreType.DMA
    result = pl.pallas_call(
        functools.partial(kernel, n, ny, nz, count, pair, fused),
        out_shape=jax.ShapeDtypeStruct((rows, own_width), BF16),
        in_specs=[pl.BlockSpec(memory_space=pltpu.VMEM)] + [pl.BlockSpec(memory_space=pl.ANY)] * 3,
        out_specs=pl.BlockSpec(memory_space=pltpu.VMEM),
        scratch_shapes=[
            pltpu.VMEM((rows, depth) if fused else (16, WIDE), BF16),
            pltpu.VMEM((2, units, part_rows, 2 * WIDE), BF16),
            pltpu.VMEM((2, units, part_rows, 2 * WIDE), BF16),
            pltpu.VMEM((2, units, part_rows, WIDE), BF16),
            pltpu.VMEM((rows, width), F32),
            pltpu.VMEM((2, 2, depth, 2 * WIDE), BF16),
            pltpu.VMEM((2, 2, pair * WIDE, width), BF16),
            *[
                pltpu.VMEM(shape if fused else (16, WIDE), BF16)
                for shape in [(PARTS, nz - 1, ny, part_rows, own_width)] * 2
                + [(PARTS, ny - 1, part_rows, own_width)] * 2
            ],
            dma((2, FLIGHT)), dma((2, units)), dma((2, FLIGHT)), dma((2, units // pair)),
            dma((2, 2, 2)), dma((2, 2)),
            dma((PARTS, ny)), dma((PARTS, ny)), dma((PARTS, nz, ny)), dma((PARTS, nz, ny)),
            dma((PARTS, nz)), dma((PARTS, nz)), dma((PARTS, ny)), dma((PARTS, ny)),
        ],
        compiler_params=pltpu.CompilerParams(
            collective_id=0, has_side_effects=True, vmem_limit_bytes=60 * 2**20
        ),
    )(tokens, gate_weight, up_weight, down_weight)
    if fused:
        return result
    return lax.psum_scatter(result, ("gy", "gz"), scatter_dimension=1, tiled=True)


def solution(mesh):
    placed = (
        P("rep", ("gx", "gy", "gz")),
        P("gx", ("gy", "gz")),
        P("gx", ("gy", "gz")),
        P(("gy", "gz"), "gx"),
    )
    return jax.shard_map(
        functools.partial(body, mesh.shape["gx"], mesh.shape["gy"], mesh.shape["gz"]),
        mesh=mesh, in_specs=placed, out_specs=P("rep", ("gx", "gy", "gz")), check_vma=False,
    )
```
